32 devices in a mesh: seq: 4 (over y, x), grp: 8 (over z, core).
Axes of the slice: x: 2, y: 2, z: 4, core: 2. Of those that a mesh axis runs over, the one named last changes fastest.
Arguments:
- actions: int32 [16, 7], P('grp'), may hold values from 0 to 255
- lengths: int32 [16], P('grp'), may hold values from 512 to 1024
- embed: bfloat16 [256, 4096], replicated, may hold values from -6 to 6
- attn_gain: float32 [4096], replicated, may hold values from 0.1 to 1.9
- w_query: bfloat16 [4096, 4096], P('grp', 'seq'), may hold values from -0.09375 to 0.09375
- w_key: bfloat16 [4096, 4096], P('grp', 'seq'), may hold values from -0.140625 to 0.140625
- w_value: bfloat16 [4096, 4096], P('grp', 'seq'), may hold values from -0.09375 to 0.09375
- w_out: bfloat16 [4096, 4096], P('grp', 'seq'), may hold values from -0.09375 to 0.09375
- key_cache: bfloat16 [16, 1024, 4096], P('grp', 'seq'), may hold values from -136 to 136
- value_cache: bfloat16 [16, 1024, 4096], P('grp', 'seq'), may hold values from -6 to 6
- final_gain: float32 [4096], replicated, may hold values from 0.1 to 1.9
- head: bfloat16 [256, 4096], P('seq'), may hold values from -0.25 to 0.25
Outputs:
- logprob: float32 [16, 7, 256], P('grp', None, 'seq')
The draws below stay inside these ranges and needn't reach their ends.
Inputs may be any that keep to these rules, and one draw needn't show every extreme that they name: Robot r's prompt occupies cache positions 0 to lengths[r] - 1.
All inputs are finite; a program needn't handle non-finite values.
Results may differ from the reference program's by a relative error of at most 0.008.
Values may be sent and summed in bfloat16 or wider, within the bound.
A program may use at most 64 MiB of HBM per device.

```python
import jax
import jax.numpy as jnp
from jax import lax

D = 4096
HEADS = 32
HEAD_DIM = 128
BINS = 256
STEPS = 7
ROBOTS = 16
PROMPT = 1024


def projection_pair(key):
    first, second = jax.random.split(jax.random.fold_in(key, 29), 2)
    scale = D ** (-0.5)
    query_part = jnp.clip(jax.random.normal(first, (D, D), jnp.float32), -6.0, 6.0) * scale
    noise_part = jnp.clip(jax.random.normal(second, (D, D), jnp.float32), -6.0, 6.0) * scale
    key_part = 0.75 * query_part + 0.66 * noise_part
    return (query_part, key_part)


def draw_w_query(key, part):
    query_part, key_part = projection_pair(key)
    return query_part.astype(jnp.bfloat16)


def draw_w_key(key, part):
    query_part, key_part = projection_pair(key)
    return key_part.astype(jnp.bfloat16)


def draw_key_cache(key, part):
    first = jax.random.fold_in(jax.random.fold_in(key, 17), 0)
    base = jnp.clip(jax.random.normal(first, (ROBOTS, PROMPT, D), jnp.float32), -6.0, 6.0)
    return base.astype(jnp.bfloat16)


def touch_ends(result, own_key, low, high):
    dims = result.shape
    place = [jax.random.randint(jax.random.fold_in(own_key, axis), (), 0, dims[axis]) for axis in range(len(dims))]
    result = result.at[tuple(place)].set(low)
    longest = dims.index(max(dims))
    place[longest] = (place[longest] + 1) % dims[longest]
    return result.at[tuple(place)].set(high)


def level_of(own_key, extent, cuts, smallest, high):
    factor_of = 1.0
    for dim, shards_of in cuts:
        heights = jax.random.uniform(jax.random.fold_in(jax.random.fold_in(own_key, 6), dim), (shards_of,), jnp.float32, smallest / len(cuts), high / len(cuts))
        factor_of = factor_of * jnp.repeat(jnp.exp(heights), extent[dim] // shards_of).reshape((-1,) + (1,) * (len(extent) - 1 - dim))
    return factor_of


def normal_values(own_key, dims, width, limit, cuts=(), kind=jnp.bfloat16):
    level = level_of(own_key, dims, cuts, -0.22, 0.18) if cuts else 1.0
    entries = jax.random.normal(own_key, dims, jnp.float32) * width * level
    return jnp.minimum(jnp.maximum(entries, -limit), limit).astype(kind)


def setup_inputs(seed: int = 0) -> dict:
    splits = jax.random.split(jax.random.key(seed), 13)
    actions = touch_ends(jax.random.randint(splits[0], (ROBOTS, STEPS), 0, BINS), jax.random.fold_in(splits[0], 1), 0, BINS - 1).astype(jnp.int32)
    lengths = touch_ends(jax.random.randint(splits[1], (ROBOTS,), PROMPT // 2, PROMPT + 1), jax.random.fold_in(splits[1], 1), PROMPT // 2, PROMPT).astype(jnp.int32)
    embed = normal_values(splits[2], (BINS, D), 1.0, 6.0)
    attn_gain = jnp.clip(1.0 + 0.18 * jax.random.normal(splits[3], (D,), jnp.float32), 0.1, 1.9)
    w_query = draw_w_query(jax.random.fold_in(splits[12], 71), 0)
    w_key = draw_w_key(jax.random.fold_in(splits[12], 71), 0)
    w_value = normal_values(splits[6], (D, D), D ** -0.5, 0.09375, ((0, 8), (1, 4)))
    w_out = normal_values(splits[7], (D, D), D ** -0.5, 0.09375, ((0, 8), (1, 4)))
    key_cache = draw_key_cache(jax.random.fold_in(splits[12], 71), 0)
    value_cache = normal_values(splits[9], (ROBOTS, PROMPT, D), 1.0, 6.0, ((0, 8), (1, 4)))
    final_gain = jnp.clip(1.0 + 0.18 * jax.random.normal(splits[10], (D,), jnp.float32), 0.1, 1.9)
    head = normal_values(splits[11], (BINS, D), (D // 9) ** -0.5, 0.25, ((0, 4),))
    return dict(actions=actions, lengths=lengths, embed=embed, attn_gain=attn_gain, w_query=w_query, w_key=w_key, w_value=w_value, w_out=w_out, key_cache=key_cache, value_cache=value_cache, final_gain=final_gain, head=head)


def rms_scale(values, gain):
    mean_square = lax.optimization_barrier(jnp.mean(values * values, axis=-1, keepdims=True))
    return values * lax.rsqrt(mean_square + 1e-05) * gain

def rotate(values, places):
    half = values.shape[-1] // 2
    freq = 10000.0 ** (-(jnp.arange(half, dtype=jnp.float32) * 2.0 / values.shape[-1]))
    angle = places[..., None, None] * freq
    first = values[..., :half]
    second = values[..., half:]
    cosine = jnp.cos(angle)
    sine = jnp.sin(angle)
    return jnp.concatenate([first * cosine - second * sine, second * cosine + first * sine], axis=-1)

def reference(actions, lengths, embed, attn_gain, w_query, w_key, w_value, w_out, key_cache, value_cache, final_gain, head):
    bins = jnp.arange(BINS, dtype=jnp.int32)
    onehot = (actions[:, :, None] == bins[None, None, :]).astype(jnp.float32)
    inputs = jnp.einsum('rtb,bd->rtd', onehot, embed.astype(jnp.float32))
    normed = rms_scale(inputs, attn_gain).astype(jnp.bfloat16).reshape(ROBOTS * STEPS, D)
    places = (lengths[:, None] + jnp.arange(STEPS, dtype=jnp.int32)[None, :]).astype(jnp.float32)

    def heads_of(flat):
        return flat.reshape(ROBOTS, STEPS, HEADS, HEAD_DIM)
    query = rotate(heads_of(jnp.dot(normed, w_query, preferred_element_type=jnp.float32)), places).astype(jnp.bfloat16)
    key = rotate(heads_of(jnp.dot(normed, w_key, preferred_element_type=jnp.float32)), places).astype(jnp.bfloat16)
    value = heads_of(jnp.dot(normed, w_value, preferred_element_type=jnp.float32)).astype(jnp.bfloat16)
    scale = HEAD_DIM ** (-0.5)
    prompt_index = jnp.arange(PROMPT, dtype=jnp.int32)
    step_index = jnp.arange(STEPS, dtype=jnp.int32)
    causal = step_index[None, :] <= step_index[:, None]

    def one_robot(items):
        query_r, key_r, value_r, cache_k, cache_v, length = items
        query_f = query_r.astype(jnp.float32)
        cache_k = cache_k.reshape(PROMPT, HEADS, HEAD_DIM).astype(jnp.float32)
        cache_v = cache_v.reshape(PROMPT, HEADS, HEAD_DIM).astype(jnp.float32)
        valid = prompt_index < length
        prompt_scores = jnp.einsum('thd,phd->thp', query_f, cache_k) * scale
        window_scores = jnp.einsum('thd,jhd->thj', query_f, key_r.astype(jnp.float32)) * scale
        prompt_scores = jnp.where(valid[None, None, :], prompt_scores, -1e+30)
        window_scores = jnp.where(causal[:, None, :], window_scores, -1e+30)
        top = jnp.maximum(lax.optimization_barrier(jnp.max(prompt_scores, axis=-1)), lax.optimization_barrier(jnp.max(window_scores, axis=-1)))
        prompt_e = jnp.where(valid[None, None, :], jnp.exp(prompt_scores - top[..., None]), 0.0)
        window_e = jnp.where(causal[:, None, :], jnp.exp(window_scores - top[..., None]), 0.0)
        total = lax.optimization_barrier(jnp.sum(prompt_e, axis=-1)) + lax.optimization_barrier(jnp.sum(window_e, axis=-1))
        prompt_p = prompt_e.astype(jnp.bfloat16).astype(jnp.float32)
        window_p = window_e.astype(jnp.bfloat16).astype(jnp.float32)
        acc = jnp.einsum('thp,phd->thd', prompt_p, cache_v) + jnp.einsum('thj,jhd->thd', window_p, value_r.astype(jnp.float32))
        return (acc / total[..., None]).astype(jnp.bfloat16).reshape(STEPS, D)
    attended = lax.map(one_robot, (query, key, value, key_cache, value_cache, lengths))
    branch = jnp.dot(attended.reshape(ROBOTS * STEPS, D), w_out, preferred_element_type=jnp.float32)
    residual = inputs.reshape(ROBOTS * STEPS, D) + branch
    final = rms_scale(residual, final_gain).astype(jnp.bfloat16)
    logits = jnp.dot(final, head.T, preferred_element_type=jnp.float32)
    top = lax.optimization_barrier(jnp.max(logits, axis=-1, keepdims=True))
    logprob = logits - top - jnp.log(lax.optimization_barrier(jnp.sum(jnp.exp(logits - top), axis=-1, keepdims=True)))
    return logprob.reshape(ROBOTS, STEPS, BINS)
```

```python
import functools

import jax
import jax.numpy as jnp
from jax import lax
from jax.experimental import pallas as pl
from jax.experimental.pallas import tpu as pltpu
from jax.sharding import PartitionSpec as P

HEAD_DIM = 128
PAD = 8
MESH = pl.DeviceIdType.MESH
NEG = -1e30


def dot(a, b):
    return lax.dot_general(a, b, (((1,), (0,)), ((), ())), preferred_element_type=jnp.float32)


def dot_t(a, b):
    return lax.dot_general(a, b, (((1,), (1,)), ((), ())), preferred_element_type=jnp.float32)


def kernel(
    S,
    G,
    acts,
    lens,
    cos_ref,
    sin_ref,
    gain_ref,
    fgain_ref,
    embed_h,
    wq_h,
    wk_h,
    wv_h,
    wo_h,
    kc_h,
    vc_h,
    head_h,
    out_ref,
    embed,
    w3,
    wo,
    kc,
    vc,
    head,
    acts_all,
    part,
    got,
    kv,
    qall,
    acc_out,
    acc_in,
    st_out,
    st_in,
    att,
    attall,
    obuf,
    ogot,
    resall,
    fin,
    lse,
    load_sem,
    a_send,
    a_recv,
    b_send,
    b_recv,
    c_send,
    c_recv,
    d_send,
    d_recv,
    e_send,
    e_recv,
    f_send,
    f_recv,
    g_send,
    g_recv,
    h_send,
    h_recv,
):
    s = lax.axis_index("seq")
    g = lax.axis_index("grp")
    RW = acts.shape[0]
    robots = RW // PAD
    bins, width = embed.shape
    CB = wo.shape[1]
    RB = wo.shape[0]
    ratio = CB // RB
    LH = CB // HEAD_DIM
    pos = kc.shape[1]
    scale = HEAD_DIM ** (-0.5)

    loads = []
    for i, (src, dst) in enumerate(
        [
            (embed_h, embed),
            (wq_h, w3.at[0]),
            (wk_h, w3.at[1]),
            (wv_h, w3.at[2]),
            (kc_h, kc),
            (vc_h, vc),
            (wo_h, wo),
            (head_h, head),
        ]
    ):
        copy = pltpu.make_async_copy(src, dst, load_sem.at[i])
        copy.start()
        loads.append(copy)

    barrier = pltpu.get_barrier_semaphore()
    total_devices = S * G
    flat = s * G + g

    def greet(d, carry):
        other = lax.rem(flat + d, total_devices)
        pl.semaphore_signal(
            barrier,
            inc=1,
            device_id={"seq": other // G, "grp": lax.rem(other, G)},
            device_id_type=MESH,
        )
        return carry

    lax.fori_loop(1, total_devices, greet, 0)
    pl.semaphore_wait(barrier, total_devices - 1)

    pending = []

    def push(axis, n, me, src_of, dst, send, recv):
        copies = []
        for k in range(1, n):
            peer = lax.rem(me + k, n)
            copy = pltpu.make_async_remote_copy(
                src_ref=src_of(peer),
                dst_ref=dst,
                send_sem=send.at[k],
                recv_sem=recv.at[k],
                device_id={axis: peer},
                device_id_type=MESH,
            )
            copy.start()
            copies.append(copy)
            pending.append(copy)
        return copies

    acts_all[g] = acts[...]
    ca = push("grp", G, g, lambda p: acts, acts_all.at[g], a_send, a_recv)

    loads[0].wait()
    squares = jnp.zeros((bins, 128), jnp.float32)
    for c in range(width // 128):
        x = embed[:, c * 128 : (c + 1) * 128].astype(jnp.float32)
        squares = squares + x * x
    inv = lax.rsqrt(jnp.sum(squares, axis=-1, keepdims=True) * (1.0 / width) + 1e-05)
    block = pl.ds(pl.multiple_of(g * RB, RB), RB)
    table = (embed[:, block].astype(jnp.float32) * inv * gain_ref[:, block]).astype(jnp.bfloat16)
    for c in ca:
        c.wait_recv()
    lane_bin = lax.broadcasted_iota(jnp.int32, (G * RW, bins), 1)
    picked = acts_all[...].reshape(G * RW, 128)[:, :1]
    onehot = jnp.where(lane_bin == picked, 1.0, 0.0).astype(jnp.bfloat16)
    rows = dot(onehot, table).astype(jnp.bfloat16)
    cb = []
    for i in range(3):
        loads[1 + i].wait()
        part[i] = dot(rows, w3[i]).astype(jnp.bfloat16).reshape(G, RW, CB)
        cb.append(
            push(
                "grp", G, g, lambda p, i=i: part.at[i, p], got.at[i, g], b_send.at[i], b_recv.at[i]
            )
        )
    cols = pl.ds(pl.multiple_of(s * CB, CB), CB)
    own_hot = jnp.where(
        lax.broadcasted_iota(jnp.int32, (RW, bins), 1) == acts[:, :1], 1.0, 0.0
    ).astype(jnp.bfloat16)
    inputs = dot(own_hot, embed[:, cols])

    def summed(i):
        for c in cb[i]:
            c.wait_recv()
        total = part[i, g].astype(jnp.float32)
        for k in range(1, G):
            total = total + got[i, lax.rem(g + (G - k), G)].astype(jnp.float32)
        return total

    def rotated(x):
        parts = []
        for j in range(LH):
            y = x[:, j * HEAD_DIM : (j + 1) * HEAD_DIM]
            parts.append(y * cos_ref[...] + pltpu.roll(y, HEAD_DIM // 2, 1) * sin_ref[...])
        return jnp.concatenate(parts, axis=1).astype(jnp.bfloat16)

    qall[s] = rotated(summed(0))
    cc = push("seq", S, s, lambda p: qall.at[s], qall.at[s], c_send, c_recv)

    lane = lax.broadcasted_iota(jnp.int32, (PAD, 128), 1)
    place = lax.broadcasted_iota(jnp.int32, (PAD, pos), 1) + s * pos
    valid = [place < lens[r * PAD : (r + 1) * PAD, :1] for r in range(robots)]
    loads[4].wait()
    loads[5].wait()

    def attend(owner):
        q = qall[owner].astype(jnp.float32)
        for r in range(robots):
            low = r * PAD
            tops = jnp.zeros((PAD, 128), jnp.float32)
            totals = jnp.zeros((PAD, 128), jnp.float32)
            for j in range(LH):
                lanes = pl.ds(pl.multiple_of(owner * CB + j * HEAD_DIM, HEAD_DIM), HEAD_DIM)
                qh = q[low : low + PAD, j * HEAD_DIM : (j + 1) * HEAD_DIM].astype(jnp.bfloat16)
                score = jnp.where(valid[r], dot_t(qh, kc[r, :, lanes]) * scale, NEG)
                top = jnp.max(score, axis=-1, keepdims=True)
                e = jnp.where(valid[r], jnp.exp(score - top), 0.0)
                tops = jnp.where(lane == j, top, tops)
                totals = jnp.where(lane == j, jnp.sum(e, axis=-1, keepdims=True), totals)
                acc_out[owner, low : low + PAD, j * HEAD_DIM : (j + 1) * HEAD_DIM] = dot(
                    e.astype(jnp.bfloat16), vc[r, :, lanes]
                )
            st_out[owner, 0, low : low + PAD, :] = tops
            st_out[owner, 1, low : low + PAD, :] = totals

    attend(s)
    cd = []
    for k in range(1, S):
        cc[k - 1].wait_recv()
        owner = lax.rem(s + (S - k), S)
        attend(owner)
        for i, (src, dst) in enumerate([(acc_out, acc_in), (st_out, st_in)]):
            copy = pltpu.make_async_remote_copy(
                src_ref=src.at[owner],
                dst_ref=dst.at[s],
                send_sem=d_send.at[i, k],
                recv_sem=d_recv.at[i, k],
                device_id={"seq": owner},
                device_id_type=MESH,
            )
            copy.start()
            cd.append(copy)
            pending.append(copy)

    kv[0] = rotated(summed(1))
    kv[1] = summed(2).astype(jnp.bfloat16)
    qi = lax.broadcasted_iota(jnp.int32, (RW, RW), 0)
    kj = lax.broadcasted_iota(jnp.int32, (RW, RW), 1)
    causal = (qi // PAD == kj // PAD) & (kj <= qi)
    wide = lax.broadcasted_iota(jnp.int32, (RW, 128), 1)
    w_top = jnp.zeros((RW, 128), jnp.float32)
    w_total = jnp.zeros((RW, 128), jnp.float32)
    w_acc = []
    for j in range(LH):
        hl = slice(j * HEAD_DIM, (j + 1) * HEAD_DIM)
        score = jnp.where(causal, dot_t(qall[s, :, hl], kv[0, :, hl]) * scale, NEG)
        top = jnp.max(score, axis=-1, keepdims=True)
        e = jnp.where(causal, jnp.exp(score - top), 0.0)
        w_top = jnp.where(wide == j, top, w_top)
        w_total = jnp.where(wide == j, jnp.sum(e, axis=-1, keepdims=True), w_total)
        w_acc.append(dot(e.astype(jnp.bfloat16), kv[1, :, hl]))

    for c in cd:
        c.wait_recv()
    sources = [lax.rem(s + k, S) for k in range(1, S)]
    top = jnp.maximum(w_top, st_out[s, 0])
    for o in sources:
        top = jnp.maximum(top, st_in[o, 0])
    w_f = jnp.exp(w_top - top)
    own_f = jnp.exp(st_out[s, 0] - top)
    fs = [jnp.exp(st_in[o, 0] - top) for o in sources]
    total = w_total * w_f + st_out[s, 1] * own_f
    for o, f in zip(sources, fs):
        total = total + st_in[o, 1] * f
    for j in range(LH):
        hl = slice(j * HEAD_DIM, (j + 1) * HEAD_DIM)
        acc = w_acc[j] * w_f[:, j : j + 1] + acc_out[s, :, hl] * own_f[:, j : j + 1]
        for o, f in zip(sources, fs):
            acc = acc + acc_in[o, :, hl] * f[:, j : j + 1]
        at = j * HEAD_DIM
        att[at // RB, :, at % RB : at % RB + HEAD_DIM] = (acc / total[:, j : j + 1]).astype(
            jnp.bfloat16
        )

    home = g // ratio
    for i in range(ratio):
        for k in range(S):
            s2 = lax.rem(s + k, S)
            g2 = s * ratio + i
            if k == 0:

                @pl.when(g2 == g)
                def _():
                    attall[g] = att[i]

            def send(i=i, k=k, s2=s2, g2=g2):
                return pltpu.make_async_remote_copy(
                    src_ref=att.at[i],
                    dst_ref=attall.at[g],
                    send_sem=e_send.at[i, k],
                    recv_sem=e_recv.at[g],
                    device_id={"seq": s2, "grp": g2},
                    device_id_type=MESH,
                )

            if k == 0:

                @pl.when(g2 != g)
                def _():
                    send().start()
            else:
                send().start()

    def arrival(q):
        return pltpu.make_async_remote_copy(
            src_ref=att.at[0],
            dst_ref=attall.at[q],
            send_sem=e_send.at[0, 0],
            recv_sem=e_recv.at[q],
            device_id={"seq": s, "grp": g},
            device_id_type=MESH,
        )

    for q in range(G):

        @pl.when(jnp.logical_or(home != s, g != q))
        def _():
            arrival(q).wait_recv()

    loads[6].wait()
    loads[7].wait()
    obuf[...] = (
        dot(attall[...].reshape(G * RW, RB), wo[...]).astype(jnp.bfloat16).reshape(G, RW, CB)
    )
    cf = push("grp", G, g, lambda p: obuf.at[p], ogot.at[g], f_send, f_recv)
    for c in cf:
        c.wait_recv()
    branch = obuf[g].astype(jnp.float32)
    for k in range(1, G):
        branch = branch + ogot[lax.rem(g + k, G)].astype(jnp.float32)
    resall[s] = inputs + branch
    cg = push("seq", S, s, lambda p: resall.at[s], resall.at[s], g_send, g_recv)
    for c in cg:
        c.wait_recv()
    squares = jnp.zeros((RW, CB), jnp.float32)
    for o in range(S):
        squares = squares + resall[o] * resall[o]
    inv = lax.rsqrt(jnp.sum(squares, axis=-1, keepdims=True) * (1.0 / width) + 1e-05)
    for o in range(S):
        hl = slice(o * CB, (o + 1) * CB)
        fin[:, hl] = (resall[o] * inv * fgain_ref[:, hl]).astype(jnp.bfloat16)
    logits = dot_t(fin[...], head[...])
    row_max = jnp.max(logits, axis=-1, keepdims=True)
    row_sum = jnp.sum(jnp.exp(logits - row_max), axis=-1, keepdims=True)
    lse[s, 0] = jnp.broadcast_to(row_max, (RW, 128))
    lse[s, 1] = jnp.broadcast_to(row_sum, (RW, 128))
    ch = push("seq", S, s, lambda p: lse.at[s], lse.at[s], h_send, h_recv)
    for c in ch:
        c.wait_recv()
    top = lse[0, 0]
    for o in range(1, S):
        top = jnp.maximum(top, lse[o, 0])
    total = lse[0, 1] * jnp.exp(lse[0, 0] - top)
    for o in range(1, S):
        total = total + lse[o, 1] * jnp.exp(lse[o, 0] - top)
    out_ref[...] = logits - top[:, :1] - jnp.log(total)[:, :1]

    for c in pending:
        c.wait_send()
    for i in range(ratio):
        for k in range(S):

            def sent(i=i, k=k):
                pltpu.make_async_remote_copy(
                    src_ref=att.at[i],
                    dst_ref=attall.at[g],
                    send_sem=e_send.at[i, k],
                    recv_sem=e_recv.at[g],
                    device_id={"seq": s, "grp": g},
                    device_id_type=MESH,
                ).wait_send()

            if k == 0:

                @pl.when(s * ratio + i != g)
                def _():
                    sent()
            else:
                sent()


def on_device(
    S,
    G,
    actions,
    lengths,
    embed,
    attn_gain,
    w_query,
    w_key,
    w_value,
    w_out,
    key_cache,
    value_cache,
    final_gain,
    head,
):
    robots, steps = actions.shape
    RW = robots * PAD
    bins, width = embed.shape
    RB, CB = w_out.shape
    ratio = CB // RB
    acts = jnp.pad(actions, ((0, 0), (0, PAD - steps))).reshape(RW, 1)
    acts = jnp.broadcast_to(acts, (RW, 128))
    lens = jnp.broadcast_to(jnp.repeat(lengths, PAD)[:, None], (RW, 128))
    half = HEAD_DIM // 2
    freq = 10000.0 ** (-(jnp.arange(half, dtype=jnp.float32) * 2.0 / HEAD_DIM))
    places = (lengths[:, None] + jnp.arange(PAD, dtype=jnp.int32)[None, :]).astype(jnp.float32)
    angle = places.reshape(RW, 1) * freq
    cosine = jnp.cos(angle)
    sine = jnp.sin(angle)
    cos2 = jnp.concatenate([cosine, cosine], axis=1)
    sin2 = jnp.concatenate([-sine, sine], axis=1)
    vmem = pl.BlockSpec(memory_space=pltpu.VMEM)
    hbm = pl.BlockSpec(memory_space=pl.ANY)
    bf, f32 = jnp.bfloat16, jnp.float32
    bins_dev = head.shape[0]
    V = pltpu.VMEM
    D = pltpu.SemaphoreType.DMA
    out = pl.pallas_call(
        functools.partial(kernel, S, G),
        out_shape=jax.ShapeDtypeStruct((RW, bins_dev), f32),
        in_specs=[vmem] * 6 + [hbm] * 8,
        out_specs=vmem,
        scratch_shapes=[
            V((bins, width), bf),
            V((3, RB, CB), bf),
            V((RB, CB), bf),
            V(key_cache.shape, bf),
            V(value_cache.shape, bf),
            V(head.shape, bf),
            V((G, RW, 128), jnp.int32),
            V((3, G, RW, CB), bf),
            V((3, G, RW, CB), bf),
            V((2, RW, CB), bf),
            V((S, RW, CB), bf),
            V((S, RW, CB), f32),
            V((S, RW, CB), f32),
            V((S, 2, RW, 128), f32),
            V((S, 2, RW, 128), f32),
            V((ratio, RW, RB), bf),
            V((G, RW, RB), bf),
            V((G, RW, CB), bf),
            V((G, RW, CB), bf),
            V((S, RW, CB), f32),
            V((RW, width), bf),
            V((S, 2, RW, 128), f32),
            D((8,)),
            D((G,)),
            D((G,)),
            D((3, G)),
            D((3, G)),
            D((S,)),
            D((S,)),
            D((2, S)),
            D((2, S)),
            D((ratio, S)),
            D((G,)),
            D((G,)),
            D((G,)),
            D((S,)),
            D((S,)),
            D((S,)),
            D((S,)),
        ],
        compiler_params=pltpu.CompilerParams(
            collective_id=0, has_side_effects=True, vmem_limit_bytes=48 * 2**20
        ),
    )(
        acts,
        lens,
        cos2,
        sin2,
        attn_gain.reshape(1, width),
        final_gain.reshape(1, width),
        embed,
        w_query,
        w_key,
        w_value,
        w_out,
        key_cache,
        value_cache,
        head,
    )
    return out.reshape(robots, PAD, bins_dev)[:, :steps]


def solution(mesh):
    placed = (
        P("grp", None),
        P("grp"),
        P(),
        P(),
        P("grp", "seq"),
        P("grp", "seq"),
        P("grp", "seq"),
        P("grp", "seq"),
        P("grp", "seq", None),
        P("grp", "seq", None),
        P(),
        P("seq", None),
    )
    return jax.shard_map(
        functools.partial(on_device, mesh.shape["seq"], mesh.shape["grp"]),
        mesh=mesh,
        in_specs=placed,
        out_specs=P("grp", None, "seq"),
        check_vma=False,
    )
```

```python
import functools

import jax
import jax.numpy as jnp
from jax import lax
from jax.experimental import pallas as pl
from jax.experimental.pallas import tpu as pltpu
from jax.sharding import PartitionSpec as P

HEAD_DIM = 128
PAD = 8
MESH = pl.DeviceIdType.MESH
NEG = -1e30


def dot(a, b):
    return lax.dot_general(a, b, (((1,), (0,)), ((), ())), preferred_element_type=jnp.float32)


def dot_t(a, b):
    return lax.dot_general(a, b, (((1,), (1,)), ((), ())), preferred_element_type=jnp.float32)


def kernel(
    S,
    G,
    acts,
    lens,
    cos_ref,
    sin_ref,
    gain_ref,
    fgain_ref,
    embed_h,
    wq_h,
    wk_h,
    wv_h,
    wo_h,
    kc_h,
    vc_h,
    head_h,
    out_ref,
    embed,
    w3,
    wo,
    kc,
    vc,
    head,
    acts_all,
    part,
    got,
    kv,
    qall,
    acc_out,
    acc_in,
    st_out,
    st_in,
    att,
    attall,
    obuf,
    ogot,
    resall,
    fin,
    lse,
    load_sem,
    a_send,
    a_recv,
    b_send,
    b_recv,
    c_send,
    c_recv,
    d_send,
    d_recv,
    e_send,
    e_recv,
    f_send,
    f_recv,
    g_send,
    g_recv,
    h_send,
    h_recv,
):
    s = lax.axis_index("seq")
    g = lax.axis_index("grp")
    RW = acts.shape[0]
    robots = RW // PAD
    bins, width = embed.shape
    CB = wo.shape[1]
    RB = wo.shape[0]
    ratio = CB // RB
    LH = CB // HEAD_DIM
    pos = kc.shape[1]
    scale = HEAD_DIM ** (-0.5)

    loads = []
    for i, (src, dst) in enumerate(
        [
            (embed_h, embed),
            (wq_h, w3.at[0]),
            (wk_h, w3.at[1]),
            (wv_h, w3.at[2]),
            (kc_h, kc),
            (vc_h, vc),
            (wo_h, wo),
            (head_h, head),
        ]
    ):
        copy = pltpu.make_async_copy(src, dst, load_sem.at[i])
        loads.append(copy)
    for copy in loads[:2]:
        copy.start()

    barrier = pltpu.get_barrier_semaphore()
    total_devices = S * G
    flat = s * G + g

    def greet(d, carry):
        other = lax.rem(flat + d, total_devices)
        pl.semaphore_signal(
            barrier,
            inc=1,
            device_id={"seq": other // G, "grp": lax.rem(other, G)},
            device_id_type=MESH,
        )
        return carry

    lax.fori_loop(1, total_devices, greet, 0)
    loads[0].wait()
    for copy in loads[2:]:
        copy.start()
    squares = jnp.zeros((bins, 128), jnp.float32)
    for c in range(width // 128):
        x = embed[:, c * 128 : (c + 1) * 128].astype(jnp.float32)
        squares = squares + x * x
    pl.semaphore_wait(barrier, total_devices - 1)

    pending = []

    def push(axis, n, me, src_of, dst, send, recv):
        copies = []
        for k in range(1, n):
            peer = lax.rem(me + k, n)
            copy = pltpu.make_async_remote_copy(
                src_ref=src_of(peer),
                dst_ref=dst,
                send_sem=send.at[k],
                recv_sem=recv.at[k],
                device_id={axis: peer},
                device_id_type=MESH,
            )
            copy.start()
            copies.append(copy)
            pending.append(copy)
        return copies

    acts_all[g] = acts[...]
    ca = push("grp", G, g, lambda p: acts, acts_all.at[g], a_send, a_recv)

    inv = lax.rsqrt(jnp.sum(squares, axis=-1, keepdims=True) * (1.0 / width) + 1e-05)
    block = pl.ds(pl.multiple_of(g * RB, RB), RB)
    table = (embed[:, block].astype(jnp.float32) * inv * gain_ref[:, block]).astype(jnp.bfloat16)
    for c in ca:
        c.wait_recv()
    lane_bin = lax.broadcasted_iota(jnp.int32, (G * RW, bins), 1)
    picked = acts_all[...].reshape(G * RW, 128)[:, :1]
    onehot = jnp.where(lane_bin == picked, 1.0, 0.0).astype(jnp.bfloat16)
    rows = dot(onehot, table).astype(jnp.bfloat16)

    def push_part(i):
        return push(
            "grp", G, g, lambda p: part.at[i, p], got.at[i, g], b_send.at[i], b_recv.at[i]
        )

    cb = []
    for i in range(3):
        loads[1 + i].wait()
        part[i] = dot(rows, w3[i]).astype(jnp.bfloat16).reshape(G, RW, CB)
        if i == 0:
            cb.append(push_part(0))
    cols = pl.ds(pl.multiple_of(s * CB, CB), CB)
    own_hot = jnp.where(
        lax.broadcasted_iota(jnp.int32, (RW, bins), 1) == acts[:, :1], 1.0, 0.0
    ).astype(jnp.bfloat16)
    inputs = dot(own_hot, embed[:, cols])

    def summed(i):
        for c in cb[i]:
            c.wait_recv()
        if i == 0:
            cb.append(push_part(1))
            cb.append(push_part(2))
        total = part[i, g].astype(jnp.float32)
        for k in range(1, G):
            total = total + got[i, lax.rem(g + (G - k), G)].astype(jnp.float32)
        return total

    def rotated(x):
        parts = []
        for j in range(LH):
            y = x[:, j * HEAD_DIM : (j + 1) * HEAD_DIM]
            parts.append(y * cos_ref[...] + pltpu.roll(y, HEAD_DIM // 2, 1) * sin_ref[...])
        return jnp.concatenate(parts, axis=1).astype(jnp.bfloat16)

    qall[s] = rotated(summed(0))
    cc = push("seq", S, s, lambda p: qall.at[s], qall.at[s], c_send, c_recv)

    lane = lax.broadcasted_iota(jnp.int32, (PAD, 128), 1)
    place = lax.broadcasted_iota(jnp.int32, (PAD, pos), 1) + s * pos
    valid = [place < lens[r * PAD : (r + 1) * PAD, :1] for r in range(robots)]
    loads[4].wait()
    loads[5].wait()

    def attend(owner):
        q = qall[owner].astype(jnp.float32)
        heads = [
            pl.ds(pl.multiple_of(owner * CB + j * HEAD_DIM, HEAD_DIM), HEAD_DIM) for j in range(LH)
        ]
        raw = [
            [
                dot_t(
                    q[r * PAD : (r + 1) * PAD, j * HEAD_DIM : (j + 1) * HEAD_DIM].astype(
                        jnp.bfloat16
                    ),
                    kc[r, :, heads[j]],
                )
                for j in range(LH)
            ]
            for r in range(robots)
        ]
        for r in range(robots):
            low = r * PAD
            score = jnp.where(valid[r], jnp.stack(raw[r]) * scale, NEG)
            top = jnp.max(score, axis=-1, keepdims=True)
            e = jnp.where(valid[r], jnp.exp(score - top), 0.0)
            total = jnp.sum(e, axis=-1, keepdims=True)
            tops = jnp.zeros((PAD, 128), jnp.float32)
            totals = jnp.zeros((PAD, 128), jnp.float32)
            for j in range(LH):
                acc_out[owner, low : low + PAD, j * HEAD_DIM : (j + 1) * HEAD_DIM] = dot(
                    e[j].astype(jnp.bfloat16), vc[r, :, heads[j]]
                )
                tops = jnp.where(lane == j, top[j], tops)
                totals = jnp.where(lane == j, total[j], totals)
            st_out[owner, 0, low : low + PAD, :] = tops
            st_out[owner, 1, low : low + PAD, :] = totals

    attend(s)
    cd = []
    for k in range(1, S):
        cc[k - 1].wait_recv()
        owner = lax.rem(s + (S - k), S)
        attend(owner)
        for i, (src, dst) in enumerate([(acc_out, acc_in), (st_out, st_in)]):
            copy = pltpu.make_async_remote_copy(
                src_ref=src.at[owner],
                dst_ref=dst.at[s],
                send_sem=d_send.at[i, k],
                recv_sem=d_recv.at[i, k],
                device_id={"seq": owner},
                device_id_type=MESH,
            )
            copy.start()
            cd.append(copy)
            pending.append(copy)

    kv[0] = rotated(summed(1))
    kv[1] = summed(2).astype(jnp.bfloat16)
    qi = lax.broadcasted_iota(jnp.int32, (RW, RW), 0)
    kj = lax.broadcasted_iota(jnp.int32, (RW, RW), 1)
    causal = (qi // PAD == kj // PAD) & (kj <= qi)
    wide = lax.broadcasted_iota(jnp.int32, (RW, 128), 1)
    w_top = jnp.zeros((RW, 128), jnp.float32)
    w_total = jnp.zeros((RW, 128), jnp.float32)
    w_acc = []
    for j in range(LH):
        hl = slice(j * HEAD_DIM, (j + 1) * HEAD_DIM)
        score = jnp.where(causal, dot_t(qall[s, :, hl], kv[0, :, hl]) * scale, NEG)
        top = jnp.max(score, axis=-1, keepdims=True)
        e = jnp.where(causal, jnp.exp(score - top), 0.0)
        w_top = jnp.where(wide == j, top, w_top)
        w_total = jnp.where(wide == j, jnp.sum(e, axis=-1, keepdims=True), w_total)
        w_acc.append(dot(e.astype(jnp.bfloat16), kv[1, :, hl]))

    for c in cd:
        c.wait_recv()
    sources = [lax.rem(s + k, S) for k in range(1, S)]
    top = jnp.maximum(w_top, st_out[s, 0])
    for o in sources:
        top = jnp.maximum(top, st_in[o, 0])
    w_f = jnp.exp(w_top - top)
    own_f = jnp.exp(st_out[s, 0] - top)
    fs = [jnp.exp(st_in[o, 0] - top) for o in sources]
    total = w_total * w_f + st_out[s, 1] * own_f
    for o, f in zip(sources, fs):
        total = total + st_in[o, 1] * f
    for j in range(LH):
        hl = slice(j * HEAD_DIM, (j + 1) * HEAD_DIM)
        acc = w_acc[j] * w_f[:, j : j + 1] + acc_out[s, :, hl] * own_f[:, j : j + 1]
        for o, f in zip(sources, fs):
            acc = acc + acc_in[o, :, hl] * f[:, j : j + 1]
        at = j * HEAD_DIM
        att[at // RB, :, at % RB : at % RB + HEAD_DIM] = (acc / total[:, j : j + 1]).astype(
            jnp.bfloat16
        )

    home = g // ratio
    for i in range(ratio):
        for k in range(S):
            s2 = lax.rem(s + k, S)
            g2 = s * ratio + i
            if k == 0:

                @pl.when(g2 == g)
                def _():
                    attall[g] = att[i]

            def send(i=i, k=k, s2=s2, g2=g2):
                return pltpu.make_async_remote_copy(
                    src_ref=att.at[i],
                    dst_ref=attall.at[g],
                    send_sem=e_send.at[i, k],
                    recv_sem=e_recv.at[g],
                    device_id={"seq": s2, "grp": g2},
                    device_id_type=MESH,
                )

            if k == 0:

                @pl.when(g2 != g)
                def _():
                    send().start()
            else:
                send().start()

    def arrival(q):
        return pltpu.make_async_remote_copy(
            src_ref=att.at[0],
            dst_ref=attall.at[q],
            send_sem=e_send.at[0, 0],
            recv_sem=e_recv.at[q],
            device_id={"seq": s, "grp": g},
            device_id_type=MESH,
        )

    for q in range(G):

        @pl.when(jnp.logical_or(home != s, g != q))
        def _():
            arrival(q).wait_recv()

    loads[6].wait()
    loads[7].wait()
    obuf[...] = (
        dot(attall[...].reshape(G * RW, RB), wo[...]).astype(jnp.bfloat16).reshape(G, RW, CB)
    )
    cf = push("grp", G, g, lambda p: obuf.at[p], ogot.at[g], f_send, f_recv)
    for c in cf:
        c.wait_recv()
    branch = obuf[g].astype(jnp.float32)
    for k in range(1, G):
        branch = branch + ogot[lax.rem(g + k, G)].astype(jnp.float32)
    resall[s] = inputs + branch
    cg = push("seq", S, s, lambda p: resall.at[s], resall.at[s], g_send, g_recv)
    for c in cg:
        c.wait_recv()
    squares = jnp.zeros((RW, CB), jnp.float32)
    for o in range(S):
        squares = squares + resall[o] * resall[o]
    inv = lax.rsqrt(jnp.sum(squares, axis=-1, keepdims=True) * (1.0 / width) + 1e-05)
    for o in range(S):
        hl = slice(o * CB, (o + 1) * CB)
        fin[:, hl] = (resall[o] * inv * fgain_ref[:, hl]).astype(jnp.bfloat16)
    logits = dot_t(fin[...], head[...])
    row_max = jnp.max(logits, axis=-1, keepdims=True)
    row_sum = jnp.sum(jnp.exp(logits - row_max), axis=-1, keepdims=True)
    lse[s, 0] = jnp.broadcast_to(row_max, (RW, 128))
    lse[s, 1] = jnp.broadcast_to(row_sum, (RW, 128))
    ch = push("seq", S, s, lambda p: lse.at[s], lse.at[s], h_send, h_recv)
    for c in ch:
        c.wait_recv()
    top = lse[0, 0]
    for o in range(1, S):
        top = jnp.maximum(top, lse[o, 0])
    total = lse[0, 1] * jnp.exp(lse[0, 0] - top)
    for o in range(1, S):
        total = total + lse[o, 1] * jnp.exp(lse[o, 0] - top)
    out_ref[...] = logits - top[:, :1] - jnp.log(total)[:, :1]

    for c in pending:
        c.wait_send()
    for i in range(ratio):
        for k in range(S):

            def sent(i=i, k=k):
                pltpu.make_async_remote_copy(
                    src_ref=att.at[i],
                    dst_ref=attall.at[g],
                    send_sem=e_send.at[i, k],
                    recv_sem=e_recv.at[g],
                    device_id={"seq": s, "grp": g},
                    device_id_type=MESH,
                ).wait_send()

            if k == 0:

                @pl.when(s * ratio + i != g)
                def _():
                    sent()
            else:
                sent()


def on_device(
    S,
    G,
    actions,
    lengths,
    embed,
    attn_gain,
    w_query,
    w_key,
    w_value,
    w_out,
    key_cache,
    value_cache,
    final_gain,
    head,
):
    robots, steps = actions.shape
    RW = robots * PAD
    bins, width = embed.shape
    RB, CB = w_out.shape
    ratio = CB // RB
    acts = jnp.pad(actions, ((0, 0), (0, PAD - steps))).reshape(RW, 1)
    acts = jnp.broadcast_to(acts, (RW, 128))
    lens = jnp.broadcast_to(jnp.repeat(lengths, PAD)[:, None], (RW, 128))
    half = HEAD_DIM // 2
    freq = 10000.0 ** (-(jnp.arange(half, dtype=jnp.float32) * 2.0 / HEAD_DIM))
    places = (lengths[:, None] + jnp.arange(PAD, dtype=jnp.int32)[None, :]).astype(jnp.float32)
    angle = places.reshape(RW, 1) * freq
    cosine = jnp.cos(angle)
    sine = jnp.sin(angle)
    cos2 = jnp.concatenate([cosine, cosine], axis=1)
    sin2 = jnp.concatenate([-sine, sine], axis=1)
    vmem = pl.BlockSpec(memory_space=pltpu.VMEM)
    hbm = pl.BlockSpec(memory_space=pltpu.HBM)
    bf, f32 = jnp.bfloat16, jnp.float32
    bins_dev = head.shape[0]
    V = pltpu.VMEM
    D = pltpu.SemaphoreType.DMA
    out = pl.pallas_call(
        functools.partial(kernel, S, G),
        out_shape=jax.ShapeDtypeStruct((RW, bins_dev), f32),
        in_specs=[vmem] * 6 + [hbm] * 8,
        out_specs=vmem,
        scratch_shapes=[
            V((bins, width), bf),
            V((3, RB, CB), bf),
            V((RB, CB), bf),
            V(key_cache.shape, bf),
            V(value_cache.shape, bf),
            V(head.shape, bf),
            V((G, RW, 128), jnp.int32),
            V((3, G, RW, CB), bf),
            V((3, G, RW, CB), bf),
            V((2, RW, CB), bf),
            V((S, RW, CB), bf),
            V((S, RW, CB), f32),
            V((S, RW, CB), f32),
            V((S, 2, RW, 128), f32),
            V((S, 2, RW, 128), f32),
            V((ratio, RW, RB), bf),
            V((G, RW, RB), bf),
            V((G, RW, CB), bf),
            V((G, RW, CB), bf),
            V((S, RW, CB), f32),
            V((RW, width), bf),
            V((S, 2, RW, 128), f32),
            D((8,)),
            D((G,)),
            D((G,)),
            D((3, G)),
            D((3, G)),
            D((S,)),
            D((S,)),
            D((2, S)),
            D((2, S)),
            D((ratio, S)),
            D((G,)),
            D((G,)),
            D((G,)),
            D((S,)),
            D((S,)),
            D((S,)),
            D((S,)),
        ],
        compiler_params=pltpu.CompilerParams(
            collective_id=0, has_side_effects=True, vmem_limit_bytes=56 * 2**20
        ),
    )(
        acts,
        lens,
        cos2,
        sin2,
        attn_gain.reshape(1, width),
        final_gain.reshape(1, width),
        embed,
        w_query,
        w_key,
        w_value,
        w_out,
        key_cache,
        value_cache,
        head,
    )
    return out.reshape(robots, PAD, bins_dev)[:, :steps]


def solution(mesh):
    placed = (
        P("grp", None),
        P("grp"),
        P(),
        P(),
        P("grp", "seq"),
        P("grp", "seq"),
        P("grp", "seq"),
        P("grp", "seq"),
        P("grp", "seq", None),
        P("grp", "seq", None),
        P(),
        P("seq", None),
    )
    return jax.shard_map(
        functools.partial(on_device, mesh.shape["seq"], mesh.shape["grp"]),
        mesh=mesh,
        in_specs=placed,
        out_specs=P("grp", None, "seq"),
        check_vma=False,
    )
```
